512 devices in a mesh: rep: 16 (over z, x_lo), fsdp: 32 (over x_hi, y, core).
Axes of the slice: x: 4 (x_hi: 2, x_lo: 2; x = x_hi * 2 + x_lo), y: 8, z: 8, core: 2. Of those that a mesh axis runs over, the one named last changes fastest.
Arguments:
- cotangent: bfloat16 [163840, 4096], P(('rep', 'fsdp')), may hold values from -6 to 6
- gate_pre: bfloat16 [163840, 256], P(('rep', 'fsdp')), may hold values from -6 to 6
- up_pre: bfloat16 [163840, 256], P(('rep', 'fsdp')), may hold values from -24 to 24
- slab_weight: bfloat16 [256, 4096], P('fsdp'), may hold values from -0.09375 to 0.09375
- base_params: float32 [256, 4096], P('fsdp'), may hold values from -6 to 6
- momentum: float32 [2, 256, 4096], P(None, 'fsdp'), may hold values from -4 to 4
- codes: int32 [16, 256, 4096], P('rep', 'fsdp'), may hold values from -8 to 7
- scales: float32 [16, 256, 32], P('rep', 'fsdp'), may hold values from 0.05 to 0.5
- frag_index: int32 [1], replicated, may hold values from 0 to 1
Outputs:
- inner_grad: float32 [16, 256, 4096], P('rep', 'fsdp')
- grad_gate: bfloat16 [163840, 256], P(('rep', 'fsdp'))
- grad_up: bfloat16 [163840, 256], P(('rep', 'fsdp'))
- new_params: float32 [256, 4096], P('fsdp')
- new_momentum: float32 [256, 4096], P('fsdp')
The draws below stay inside these ranges and needn't reach their ends.
All inputs are finite; a program needn't handle non-finite values.
Results may differ from the reference program's by a relative error of at most 0.0029.
Values may be sent and summed in bfloat16 or wider, within the bound.
No kernel may reach another device: no remote copies, remote signals or barrier semaphores. Data moves between devices by JAX's collectives and lax.ppermute only.
A program may use at most 64 MiB of HBM per device.

```python
import math
import jax
import jax.numpy as jnp
from jax import lax

D = 4096
SLAB = 256
NFRAG = 2
REPLICAS = 16
TOK_REP = 10240
TOKENS = 163840
FROWS = 256


def with_ends(result, stream_key, smallest, high):
    spot = [jax.random.randint(jax.random.fold_in(stream_key, axis), (), 0, length) for axis, length in enumerate(result.shape)]
    widest = result.shape.index(max(result.shape))
    beside = spot[:widest] + [(spot[widest] + 1) % result.shape[widest]] + spot[widest + 1:]
    return result.at[tuple(spot)].set(smallest).at[tuple(beside)].set(high)


def spiked(drawn, rng, source, target, blocks, factor):
    owner, partner = [(jnp.arange(drawn.shape[position]) // (drawn.shape[position] // blocks)).reshape([-1 if axis == position else 1 for axis in range(drawn.ndim)]) for position in (source, target)]
    chosen = jax.random.permutation(rng, blocks)[partner]
    strong = (owner == chosen) | (owner == (partner + blocks // 2) % blocks)
    return jnp.where(strong, factor * drawn, drawn)


def level_of(stream_key, extent, split, least, high):
    level, own = 1.0, jax.random.fold_in(stream_key, 6)
    for dim, blocks in split:
        draws = jnp.exp(jax.random.uniform(jax.random.fold_in(own, dim), (blocks,), jnp.float32, least / len(split), high / len(split)))
        level = level * jnp.repeat(draws, extent[dim] // blocks).reshape([-1 if axis == dim else 1 for axis in range(len(extent))])
    return level


def scatter_about(key, extent, scale, most, pieces=(), dtype=jnp.bfloat16):
    values = jax.random.normal(key, extent, jnp.float32) * scale
    if len(pieces) > 0:
        values = level_of(key, extent, pieces, -0.22, 0.18) * values
    return jnp.clip(values, min=-most, max=most).astype(dtype)


def gaussian_with(own_key, shape, deviation, most, split, heavy, dtype=jnp.bfloat16):
    result = deviation * jax.random.normal(own_key, shape, jnp.float32)
    if split:
        result = result * level_of(own_key, shape, split, -0.22, 0.18)
    return jnp.clip(spiked(result, jax.random.fold_in(own_key, 3), *heavy), -most, most).astype(dtype)


def setup_inputs(seed: int = 0) -> dict:
    seeds = jax.random.split(jax.random.key(seed), 10)
    cotangent = scatter_about(seeds[0], (TOKENS, D), 1.0, 6.0, ((0, 512),))
    gate_pre = scatter_about(seeds[1], (TOKENS, SLAB), 1.0, 6.0, ((0, 512),))
    up_pre = gaussian_with(seeds[2], (TOKENS, SLAB), 1.0, 24.0, ((0, 512),), (0, 1, 256, 6.0))
    slab_weight = scatter_about(seeds[3], (SLAB, D), D ** -0.5, 0.09375, ((0, 32),))
    base_params = scatter_about(seeds[4], (FROWS, D), 1.0, 6.0, ((0, 32),), jnp.float32)
    momentum = scatter_about(seeds[5], (NFRAG, FROWS, D), 0.5, 4.0, ((1, 32),), jnp.float32)
    codes = with_ends(jax.random.randint(seeds[6], (REPLICAS, FROWS, D), -8, 8), jax.random.fold_in(seeds[6], 1), -8, 7).astype(jnp.int32)
    scales = jnp.clip(jnp.exp(math.log(0.5) - 2.3025851 * jax.random.uniform(seeds[7], (REPLICAS, FROWS, D // 128), jnp.float32) ** level_of(seeds[7], (REPLICAS, FROWS, D // 128), ((0, 16), (1, 32)), -0.2, 0.2)), 0.05, 0.5)
    frag_index = jax.random.randint(seeds[8], (1,), 0, NFRAG).astype(jnp.int32)
    return {"cotangent": cotangent, "gate_pre": gate_pre, "up_pre": up_pre, "slab_weight": slab_weight, "base_params": base_params, "momentum": momentum, "codes": codes, "scales": scales, "frag_index": frag_index}


def reference(cotangent, gate_pre, up_pre, slab_weight, base_params, momentum, codes, scales, frag_index):
    gate = gate_pre.astype(jnp.float32)
    upper = up_pre.astype(jnp.float32)
    silu_gate = jax.nn.silu(gate)
    hidden = (silu_gate * upper).astype(jnp.bfloat16)
    grad_hidden = jnp.dot(cotangent, slab_weight.T, preferred_element_type=jnp.float32)
    sigma = jax.nn.sigmoid(gate)
    grad_up = (grad_hidden * silu_gate).astype(jnp.bfloat16)
    grad_gate = (grad_hidden * upper * sigma * (1.0 + gate * (1.0 - sigma))).astype(jnp.bfloat16)
    hid_three = hidden.reshape(REPLICAS, TOK_REP, SLAB)
    cot_three = cotangent.reshape(REPLICAS, TOK_REP, D)
    factor = 1.0 / math.sqrt(TOK_REP)

    def one_group(pair):
        hid_group, cot_group = pair
        total = jnp.dot(hid_group.T, cot_group, preferred_element_type=jnp.float32)
        return total * factor
    inner_grad = lax.map(one_group, (hid_three, cot_three))
    blocks = codes.astype(jnp.float32).reshape(REPLICAS, FROWS, D // 128, 128) * scales[..., None]
    mean_delta = lax.optimization_barrier(jnp.sum(blocks, axis=0)).reshape(FROWS, D) / REPLICAS
    old_momentum = lax.dynamic_index_in_dim(momentum, frag_index[0], 0, keepdims=False)
    new_momentum = 0.9 * old_momentum + mean_delta
    new_params = base_params - 0.7 * (mean_delta + 0.9 * new_momentum)
    return (inner_grad, grad_gate, grad_up, new_params, new_momentum)
```

```python
import math

import jax
import jax.numpy as jnp
from jax import lax
from jax.sharding import Mesh, PartitionSpec as P

REP = ("z", "xl")
FSDP = ("xh", "y", "core")
OFFSETS = (-3, 0, 3, -2, 1, 4, -1, 2)


def shift(value, axis, step):
    n = lax.axis_size(axis)
    return lax.ppermute(value, axis, [(i, (i + step) % n) for i in range(n)])


def swap(value, axis, bit=1):
    n = lax.axis_size(axis)
    return lax.ppermute(value, axis, [(i, i ^ bit) for i in range(n)])


def chunk_owner(core_rel, y_offset, x_rel):
    x = lax.axis_index("xh") ^ x_rel
    y = (lax.axis_index("y") + y_offset) % 8
    core = lax.axis_index("core") ^ core_rel
    return (x * 8 + y) * 2 + core


def selector(order):
    owners = jnp.stack([chunk_owner(*place) for place in order])
    rows = (owners[:, None] * 8 + jnp.arange(8)[None, :]).reshape(256, 1)
    return (rows == jnp.arange(256)[None, :]).astype(jnp.bfloat16)


def outer_update(summed, replicas, old_momentum, base_rows):
    mean_delta = summed / replicas
    new_momentum = 0.9 * old_momentum + mean_delta
    new_params = base_rows - 0.7 * (mean_delta + 0.9 * new_momentum)
    return (new_params, new_momentum)


def gather_rows(w):
    w = jnp.concatenate([w, swap(w, "xh")])
    up, down = shift(w, "y", 3), shift(w, "y", -3)
    own = jnp.concatenate([up, w, down])
    from_above = shift(own, "y", -1)
    from_below = shift(own[16:], "y", 1)
    half = jnp.concatenate([own, from_above, from_below])
    return jnp.concatenate([half, swap(half, "core")])


def reduce_rows(part):
    bf16 = jnp.bfloat16
    s = part[:128] + swap(part[128:].astype(bf16), "core").astype(jnp.float32)
    s = s[:64] + swap(s[64:].astype(bf16), "xh").astype(jnp.float32)
    to_up, to_down = s[24:48].astype(bf16), s[48:].astype(bf16)
    below, above = shift(to_up, "y", 1), shift(to_down, "y", -1)
    t = s[:24] + below.astype(jnp.float32)
    t = jnp.concatenate([t[:8], t[8:] + above.astype(jnp.float32)])
    far_up = shift(t[16:].astype(bf16), "y", 3)
    far_down = shift(t[:8].astype(bf16), "y", -3)
    return t[8:16] + far_up.astype(jnp.float32) + far_down.astype(jnp.float32)


def sum_replicas(delta):
    s = delta + swap(delta, "xl")
    for bit in (1, 2, 4):
        s = s + swap(s, "z", bit)
    return s


def per_device(
    cotangent, gate_pre, up_pre, slab_weight, base_params, momentum, codes, scales, frag_index
):
    gate = gate_pre.astype(jnp.float32)
    upper = up_pre.astype(jnp.float32)
    silu_gate = jax.nn.silu(gate)
    hidden = (silu_gate * upper).astype(jnp.bfloat16)
    frag_rows = codes.shape[1]
    width = codes.shape[2]
    blocks = (
        codes[0].astype(jnp.float32).reshape(frag_rows, width // 128, 128) * scales[0][..., None]
    )
    local_delta = blocks.reshape(frag_rows, width)
    old_momentum = lax.dynamic_index_in_dim(momentum, frag_index[0], 0, keepdims=False)
    summed = sum_replicas(local_delta)
    new_params, new_momentum = outer_update(summed, 16, old_momentum, base_params)

    pick = selector([(c, o, x) for c in (0, 1) for x in (0, 1) for o in OFFSETS])
    hidden_rel = jnp.dot(hidden, pick.T)
    part = lax.dot_general(
        hidden_rel, cotangent, (((0,), (0,)), ((), ())), preferred_element_type=jnp.float32
    )
    factor = 1.0 / math.sqrt(10240)
    inner_grad = (reduce_rows(part) * factor)[None]

    place = selector([(c, o, x) for c in (0, 1) for o in OFFSETS for x in (0, 1)])
    weight = jnp.dot(place.T, gather_rows(slab_weight))
    grad_hidden = jnp.einsum("td,rd->tr", cotangent, weight, preferred_element_type=jnp.float32)
    sigma = jax.nn.sigmoid(gate)
    grad_up = (grad_hidden * silu_gate).astype(jnp.bfloat16)
    grad_gate = (grad_hidden * upper * sigma * (1.0 + gate * (1.0 - sigma))).astype(jnp.bfloat16)
    return (inner_grad, grad_gate, grad_up, new_params, new_momentum)


def solution(mesh):
    fine = Mesh(mesh.devices.reshape(8, 2, 2, 8, 2), REP + FSDP)
    tokens = P(REP + FSDP, None)
    return jax.shard_map(
        per_device,
        mesh=fine,
        in_specs=(
            tokens,
            tokens,
            tokens,
            P(FSDP, None),
            P(FSDP, None),
            P(None, FSDP, None),
            P(REP, FSDP, None),
            P(REP, FSDP, None),
            P(),
        ),
        out_specs=(P(REP, FSDP, None), tokens, tokens, P(FSDP, None), P(FSDP, None)),
        check_vma=False,
    )
```

```python
import functools
import math

import jax
import jax.numpy as jnp
from jax import lax
from jax.experimental import pallas as pl
from jax.experimental.pallas import tpu as pltpu
from jax.sharding import Mesh, PartitionSpec as P

REP = ("z", "xl")
FSDP = ("xh", "y", "core")
BF16 = jnp.bfloat16
F32 = jnp.float32
STEP = 2048


def shift(value, axis, step):
    n = lax.axis_size(axis)
    return lax.ppermute(value, axis, [(i, (i + step) % n) for i in range(n)])


def swap(value, axis, bit=1):
    n = lax.axis_size(axis)
    return lax.ppermute(value, axis, [(i, i ^ bit) for i in range(n)])


def picker(first, count):
    place = lax.broadcasted_iota(jnp.int32, (count, 256), 0) + first
    row = lax.broadcasted_iota(jnp.int32, (count, 256), 1)
    core = lax.axis_index("core") ^ (place >> 7)
    x = lax.axis_index("xh") ^ ((place >> 6) & 1)
    y = lax.axis_index("y") ^ ((place >> 5) & 1) ^ ((place >> 3) & 2) ^ ((place >> 1) & 4)
    wanted = (((x * 8 + y) * 2 + core) << 3) + (place & 7)
    return jnp.where(wanted == row, 1.0, 0.0).astype(BF16)


def across(a, b):
    return lax.dot_general(a, b, (((1,), (1,)), ((), ())), preferred_element_type=F32)


def fetch(copies):
    for copy in copies:
        copy.start()


def chunk_copies(cot, held, sems):
    return [
        pltpu.make_async_copy(
            cot.at[:, pl.ds(i * STEP, STEP)], held.at[:, pl.ds(i * STEP, STEP)], sems.at[i]
        )
        for i in range(held.shape[1] // STEP)
    ]


def part_kernel(cot, gate, up, send, keep, held, gate_held, up_held, sems, small_sems):
    small = [
        pltpu.make_async_copy(gate, gate_held, small_sems.at[0]),
        pltpu.make_async_copy(up, up_held, small_sems.at[1]),
    ]
    large = chunk_copies(cot, held, sems)
    fetch(small + large)
    pick = picker(0, 256)
    for copy in small:
        copy.wait()
    g = across(pick, gate_held[...])
    hidden = (g / (1.0 + jnp.exp(-g)) * across(pick, up_held[...])).astype(BF16)
    for i, copy in enumerate(large):
        copy.wait()
        here = pl.ds(i * STEP, STEP)
        total = jnp.dot(hidden, held[:, here], preferred_element_type=F32)
        keep[:, here] = total[:128]
        send[:, here] = total[128:].astype(BF16)


def add_kernel(keep, got, send, left):
    left[...] = keep[:64] + got[:64].astype(F32)
    send[...] = (keep[64:] + got[64:].astype(F32)).astype(BF16)


def factor_kernel(gate, up, by_gate, by_up):
    pick = picker(0, 256)
    g = across(gate[...], pick)
    u = across(up[...], pick)
    sigma = 1.0 / (1.0 + jnp.exp(-g))
    by_up[...] = g * sigma
    by_gate[...] = u * sigma * (1.0 + g * (1.0 - sigma))


def half_kernel(cot, mine, grad):
    grad[...] = across(cot[...], mine[...])


def grad_kernel(cot, other, grad, by_gate, by_up, grad_gate, grad_up):
    pick = picker(0, 256)
    total = jnp.concatenate([grad[...], across(cot[...], other[...])], axis=1)
    du = (total * by_up[...]).astype(BF16)
    dg = (total * by_gate[...]).astype(BF16)
    grad_up[...] = jnp.dot(du, pick, preferred_element_type=F32).astype(BF16)
    grad_gate[...] = jnp.dot(dg, pick, preferred_element_type=F32).astype(BF16)


def struct(rows, columns, dtype):
    return jax.ShapeDtypeStruct((rows, columns), dtype)


def cost(macs, nbytes):
    return pl.CostEstimate(flops=2 * macs, bytes_accessed=nbytes, transcendentals=0)


def outer_update(summed, replicas, old_momentum, base_rows):
    mean_delta = summed / replicas
    new_momentum = 0.9 * old_momentum + mean_delta
    new_params = base_rows - 0.7 * (mean_delta + 0.9 * new_momentum)
    return (new_params, new_momentum)


def per_device(
    cotangent, gate_pre, up_pre, slab_weight, base_params, momentum, codes, scales, frag_index
):
    tokens, width = cotangent.shape
    call = functools.partial(
        pl.pallas_call, compiler_params=pltpu.CompilerParams(vmem_limit_bytes=32 << 20)
    )
    chip = pl.BlockSpec(memory_space=pltpu.VMEM)
    far = pl.BlockSpec(memory_space=pltpu.HBM)
    chunks = width // STEP

    stored = [
        pltpu.with_memory_space_constraint(a, pltpu.HBM) for a in (cotangent, gate_pre, up_pre)
    ]

    rows = codes.shape[1]
    delta = codes[0].astype(F32).reshape(rows, width // 128, 128) * scales[0][..., None]
    delta = delta.reshape(rows, width)
    w_far = swap(slab_weight, "y", 4)
    left, right = delta[:, : width // 2], delta[:, width // 2 :]
    first = lax.axis_index("xl") == 0
    delta = jnp.where(first, left, right)
    z_far = swap(jnp.where(first, right, left), "xl")

    to_core, keep = call(
        part_kernel,
        in_specs=[far, far, far],
        out_specs=[chip, chip],
        out_shape=[struct(128, width, BF16), struct(128, width, F32)],
        scratch_shapes=[
            pltpu.VMEM((tokens, width), BF16),
            pltpu.VMEM((tokens, 256), BF16),
            pltpu.VMEM((tokens, 256), BF16),
            pltpu.SemaphoreType.DMA((chunks,)),
            pltpu.SemaphoreType.DMA((2,)),
        ],
        cost_estimate=cost(256 * width * tokens, 6 << 20),
    )(*stored)
    from_core = swap(to_core, "core")
    to_x, s = call(
        add_kernel,
        in_specs=[chip, chip],
        out_specs=[chip, chip],
        out_shape=[struct(64, width, BF16), struct(64, width, F32)],
        cost_estimate=cost(128 * width, 4 << 20),
    )(keep, from_core)
    barrier = lax.optimization_barrier
    from_x = swap(to_x, "xh")
    s, w, z = barrier((s, slab_weight, delta))
    z = z + z_far
    z_far = swap(z, "z", 1)
    w = jnp.concatenate([w, w_far])
    w_far = swap(w, "y", 2)
    z = z + z_far
    s, z = barrier((s, z))
    z_far = swap(z, "z", 2)

    s = s + from_x.astype(F32)
    from_y = swap(s[32:].astype(BF16), "y", 1)
    s, w, z = barrier((s, w, z))
    w = jnp.concatenate([w, w_far])
    w_far = swap(w, "y", 1)
    z = z + z_far
    z_far = swap(z, "z", 4)

    s = s[:32] + from_y.astype(F32)
    from_y = swap(s[16:].astype(BF16), "y", 2)
    s, w, z, gate_pre, up_pre = barrier((s, w, z, gate_pre, up_pre))
    w = jnp.concatenate([w, w_far])
    w_far = swap(w, "xh")
    by_gate, by_up = call(
        factor_kernel,
        in_specs=[chip, chip],
        out_specs=[chip, chip],
        out_shape=[struct(tokens, 256, F32)] * 2,
        cost_estimate=cost(256 * 512 * tokens, 1 << 20),
    )(gate_pre, up_pre)

    s = s[:16] + from_y.astype(F32)
    from_y = swap(s[8:].astype(BF16), "y", 4)
    s, z = barrier((s, z))
    z = z + z_far

    s = s[:8] + from_y.astype(F32)
    factor = 1.0 / math.sqrt(tokens * 32)
    inner_grad = (s * factor)[None]
    z_far = swap(z, "xl")
    z = jnp.where(first, jnp.concatenate([z, z_far], axis=1), jnp.concatenate([z_far, z], axis=1))

    mine = jnp.concatenate([w, w_far])
    other = swap(mine, "core")
    grad = call(
        half_kernel,
        in_specs=[chip, chip],
        out_specs=chip,
        out_shape=struct(tokens, 128, F32),
        cost_estimate=cost(128 * width * tokens, 16 << 20),
    )(cotangent, mine)
    grad_gate, grad_up = call(
        grad_kernel,
        in_specs=[chip, chip, chip, chip, chip],
        out_specs=[chip, chip],
        out_shape=[struct(tokens, 256, BF16)] * 2,
        cost_estimate=cost(128 * width * tokens, 4 << 20),
    )(cotangent, other, grad, by_gate, by_up)

    old_momentum = lax.dynamic_index_in_dim(momentum, frag_index[0], 0, keepdims=False)
    new_params, new_momentum = outer_update(z, 16, old_momentum, base_params)
    return (inner_grad, grad_gate, grad_up, new_params, new_momentum)


def solution(mesh):
    fine = Mesh(mesh.devices.reshape(8, 2, 2, 8, 2), REP + FSDP)
    tokens = P(REP + FSDP, None)
    return jax.shard_map(
        per_device,
        mesh=fine,
        in_specs=(
            tokens,
            tokens,
            tokens,
            P(FSDP, None),
            P(FSDP, None),
            P(None, FSDP, None),
            P(REP, FSDP, None),
            P(REP, FSDP, None),
            P(),
        ),
        out_specs=(P(REP, FSDP, None), tokens, tokens, P(FSDP, None), P(FSDP, None)),
        check_vma=False,
    )
```

```python
import functools
import math

import jax
import jax.numpy as jnp
from jax import lax
from jax.experimental import pallas as pl
from jax.experimental.pallas import tpu as pltpu
from jax.sharding import Mesh, PartitionSpec as P

REP = ("z", "xl")
FSDP = ("xh", "y", "core")
BF16 = jnp.bfloat16
F32 = jnp.float32
STEP = 2048


def shift(value, axis, step):
    n = lax.axis_size(axis)
    return lax.ppermute(value, axis, [(i, (i + step) % n) for i in range(n)])


def swap(value, axis, bit=1):
    n = lax.axis_size(axis)
    return lax.ppermute(value, axis, [(i, i ^ bit) for i in range(n)])


def picker(first, count):
    place = lax.broadcasted_iota(jnp.int32, (count, 256), 0) + first
    row = lax.broadcasted_iota(jnp.int32, (count, 256), 1)
    core = lax.axis_index("core") ^ (place >> 7)
    x = lax.axis_index("xh") ^ ((place >> 6) & 1)
    y = lax.axis_index("y") ^ ((place >> 5) & 1) ^ ((place >> 3) & 2) ^ ((place >> 1) & 4)
    wanted = (((x * 8 + y) * 2 + core) << 3) + (place & 7)
    return jnp.where(wanted == row, 1.0, 0.0).astype(BF16)


def across(a, b):
    return lax.dot_general(a, b, (((1,), (1,)), ((), ())), preferred_element_type=F32)


def fetch(copies):
    for copy in copies:
        copy.start()


def chunk_copies(cot, held, sems):
    return [
        pltpu.make_async_copy(
            cot.at[:, pl.ds(i * STEP, STEP)], held.at[:, pl.ds(i * STEP, STEP)], sems.at[i]
        )
        for i in range(held.shape[1] // STEP)
    ]


def part_kernel(cot, gate, up, send, keep, held, gate_held, up_held, sems, small_sems):
    small = [
        pltpu.make_async_copy(gate, gate_held, small_sems.at[0]),
        pltpu.make_async_copy(up, up_held, small_sems.at[1]),
    ]
    large = chunk_copies(cot, held, sems)
    fetch(small + large)
    pick = picker(0, 256)
    for copy in small:
        copy.wait()
    g = across(pick, gate_held[...])
    hidden = (g / (1.0 + jnp.exp(-g)) * across(pick, up_held[...])).astype(BF16)
    for i, copy in enumerate(large):
        copy.wait()
        here = pl.ds(i * STEP, STEP)
        total = jnp.dot(hidden, held[:, here], preferred_element_type=F32)
        keep[:, here] = total[:128]
        send[:, here] = total[128:].astype(BF16)


def add_kernel(keep, got, send, left):
    left[...] = keep[:64] + got[:64].astype(F32)
    send[...] = (keep[64:] + got[64:].astype(F32)).astype(BF16)


def factor_kernel(gate, up, by_gate, by_up):
    pick = picker(0, 256)
    g = across(gate[...], pick)
    u = across(up[...], pick)
    sigma = 1.0 / (1.0 + jnp.exp(-g))
    by_up[...] = g * sigma
    by_gate[...] = u * sigma * (1.0 + g * (1.0 - sigma))


def half_kernel(cot, mine, grad):
    grad[...] = across(cot[...], mine[...])


def grad_kernel(cot, other, grad, by_gate, by_up, grad_gate, grad_up):
    pick = picker(0, 256)
    total = jnp.concatenate([grad[...], across(cot[...], other[...])], axis=1)
    du = (total * by_up[...]).astype(BF16)
    dg = (total * by_gate[...]).astype(BF16)
    grad_up[...] = jnp.dot(du, pick, preferred_element_type=F32).astype(BF16)
    grad_gate[...] = jnp.dot(dg, pick, preferred_element_type=F32).astype(BF16)


def struct(rows, columns, dtype):
    return jax.ShapeDtypeStruct((rows, columns), dtype)


def cost(macs, nbytes):
    return pl.CostEstimate(flops=2 * macs, bytes_accessed=nbytes, transcendentals=0)


def outer_update(summed, replicas, old_momentum, base_rows):
    mean_delta = summed / replicas
    new_momentum = 0.9 * old_momentum + mean_delta
    new_params = base_rows - 0.7 * (mean_delta + 0.9 * new_momentum)
    return (new_params, new_momentum)


def per_device(
    cotangent, gate_pre, up_pre, slab_weight, base_params, momentum, codes, scales, frag_index
):
    tokens, width = cotangent.shape
    call = functools.partial(
        pl.pallas_call, compiler_params=pltpu.CompilerParams(vmem_limit_bytes=16 << 20)
    )
    chip = pl.BlockSpec(memory_space=pltpu.VMEM)
    far = pl.BlockSpec(memory_space=pltpu.HBM)
    chunks = width // STEP

    stored = [
        pltpu.with_memory_space_constraint(a, pltpu.HBM) for a in (cotangent, gate_pre, up_pre)
    ]

    rows = codes.shape[1]
    delta = codes[0].astype(F32).reshape(rows, width // 128, 128) * scales[0][..., None]
    delta = delta.reshape(rows, width)
    w_far = swap(slab_weight, "y", 4)
    left, right = delta[:, : width // 2], delta[:, width // 2 :]
    first = lax.axis_index("z") % 2 == 0
    delta = jnp.where(first, left, right)
    z_far = swap(jnp.where(first, right, left), "z", 1)

    to_core, keep = call(
        part_kernel,
        in_specs=[far, far, far],
        out_specs=[chip, chip],
        out_shape=[struct(128, width, BF16), struct(128, width, F32)],
        scratch_shapes=[
            pltpu.VMEM((tokens, width), BF16),
            pltpu.VMEM((tokens, 256), BF16),
            pltpu.VMEM((tokens, 256), BF16),
            pltpu.SemaphoreType.DMA((chunks,)),
            pltpu.SemaphoreType.DMA((2,)),
        ],
        cost_estimate=cost(256 * width * tokens, 6 << 20),
    )(*stored)
    from_core = swap(to_core, "core")
    to_x, s = call(
        add_kernel,
        in_specs=[chip, chip],
        out_specs=[chip, chip],
        out_shape=[struct(64, width, BF16), struct(64, width, F32)],
        cost_estimate=cost(128 * width, 4 << 20),
    )(keep, from_core)
    barrier = lax.optimization_barrier
    from_x = swap(to_x, "xh")
    s, w, z = barrier((s, slab_weight, delta))
    z = z + z_far
    z_far = swap(z, "xl")
    w = jnp.concatenate([w, w_far])
    w_far = swap(w, "y", 2)
    z = z + z_far
    s, z = barrier((s, z))
    z_far = swap(z, "z", 2)

    s = s + from_x.astype(F32)
    from_y = swap(s[32:].astype(BF16), "y", 1)
    s, w, z = barrier((s, w, z))
    w = jnp.concatenate([w, w_far])
    w_far = swap(w, "y", 1)
    z = z + z_far
    z_far = swap(z, "z", 4)

    s = s[:32] + from_y.astype(F32)
    from_y = swap(s[16:].astype(BF16), "y", 2)
    s, w, z, gate_pre, up_pre = barrier((s, w, z, gate_pre, up_pre))
    w = jnp.concatenate([w, w_far])
    w_far = swap(w, "xh")
    by_gate, by_up = call(
        factor_kernel,
        in_specs=[chip, chip],
        out_specs=[chip, chip],
        out_shape=[struct(tokens, 256, F32)] * 2,
        cost_estimate=cost(256 * 512 * tokens, 1 << 20),
    )(gate_pre, up_pre)

    s = s[:16] + from_y.astype(F32)
    from_y = swap(s[8:].astype(BF16), "y", 4)
    s, z = barrier((s, z))
    z = z + z_far

    s = s[:8] + from_y.astype(F32)
    factor = 1.0 / math.sqrt(tokens * 32)
    inner_grad = (s * factor)[None]
    z_far = swap(z, "z", 1)
    z = jnp.where(first, jnp.concatenate([z, z_far], axis=1), jnp.concatenate([z_far, z], axis=1))

    mine = jnp.concatenate([w, w_far])
    other = swap(mine, "core")
    grad = call(
        half_kernel,
        in_specs=[chip, chip],
        out_specs=chip,
        out_shape=struct(tokens, 128, F32),
        cost_estimate=cost(128 * width * tokens, 16 << 20),
    )(cotangent, mine)
    grad_gate, grad_up = call(
        grad_kernel,
        in_specs=[chip, chip, chip, chip, chip],
        out_specs=[chip, chip],
        out_shape=[struct(tokens, 256, BF16)] * 2,
        cost_estimate=cost(128 * width * tokens, 4 << 20),
    )(cotangent, other, grad, by_gate, by_up)

    old_momentum = lax.dynamic_index_in_dim(momentum, frag_index[0], 0, keepdims=False)
    new_params, new_momentum = outer_update(z, 16, old_momentum, base_params)
    return (inner_grad, grad_gate, grad_up, new_params, new_momentum)


def solution(mesh):
    fine = Mesh(mesh.devices.reshape(8, 2, 2, 8, 2), REP + FSDP)
    tokens = P(REP + FSDP, None)
    return jax.shard_map(
        per_device,
        mesh=fine,
        in_specs=(
            tokens,
            tokens,
            tokens,
            P(FSDP, None),
            P(FSDP, None),
            P(None, FSDP, None),
            P(REP, FSDP, None),
            P(REP, FSDP, None),
            P(),
        ),
        out_specs=(P(REP, FSDP, None), tokens, tokens, P(FSDP, None), P(FSDP, None)),
        check_vma=False,
    )
```
